256 devices in a mesh: loop: 16 (over y, x_lo, core), dp: 16 (over z, x_hi).
Axes of the slice: x: 4 (x_hi: 2, x_lo: 2; x = x_hi * 2 + x_lo), y: 4, z: 8, core: 2. Of those that a mesh axis runs over, the one named last changes fastest.
Arguments:
- codes: bfloat16 [16384, 16, 1024], P(('loop', 'dp')), may hold values from -64 to 64, as said below
- cand_hidden: bfloat16 [16384, 1024], P(('loop', 'dp')), may hold values from -5 to 5, as said below
- proj: bfloat16 [1024, 1024], replicated, may hold values from -1 to 2, as said below
- gold: int32 [16384], P(('loop', 'dp')), may hold values from 0 to 1023
Outputs:
- context_loss: float32 [16384], P(('loop', 'dp'))
- code_grad: float32 [16384, 16, 1024], P(('loop', 'dp'))
- proj_grad: float32 [1024, 1024], P(('loop', 'dp'))
The draws below stay inside these ranges and needn't reach their ends.
Inputs may be any that keep to these rules, and one draw needn't show every extreme that they name: codes stay within this range. `cand_hidden`: CLS states stay within this range. `proj`: projection entries stay within this range.
All inputs are finite; a program needn't handle non-finite values.
Results may differ from the reference program's by a relative error of at most 0.0085.
Values may be sent and summed in bfloat16 or wider, within the bound.
No kernel may reach another device: no remote copies, remote signals or barrier semaphores. Data moves between devices by JAX's collectives and lax.ppermute only.
A program may use at most 128 MiB of HBM per device.

```python
import math
import jax
import jax.numpy as jnp
from jax import lax

D = 1024
M = 16
B = 64
CONTEXTS = 16384
N_LOOP = 16
N_DP = 16


def base_hidden(key):
    return jnp.clip(jax.random.normal(jax.random.fold_in(key, 7), (CONTEXTS, D), jnp.float32), -5.0, 5.0)


def draw_cand_hidden(key, part):
    return base_hidden(key).astype(jnp.bfloat16)


def draw_proj(key, part):
    noise = jnp.clip(jax.random.normal(jax.random.fold_in(key, 13), (D, D), jnp.float32), -6.0, 6.0)
    matrix = noise / math.sqrt(D)
    return matrix.astype(jnp.bfloat16)


def draw_codes(key, part):
    rough = jnp.clip(jax.random.normal(jax.random.fold_in(key, 21), (CONTEXTS, M, D), jnp.float32), -4.0, 4.0) * 4.0
    return rough.astype(jnp.bfloat16)


def set_ends(drawn, rng, low, top_value):
    place = [jax.random.randint(jax.random.fold_in(rng, axis), (), 0, length) for axis, length in enumerate(drawn.shape)]
    main_axis = drawn.shape.index(max(drawn.shape))
    neighbour = place[:main_axis] + [(place[main_axis] + 1) % drawn.shape[main_axis]] + place[main_axis + 1:]
    return drawn.at[tuple(place)].set(low).at[tuple(neighbour)].set(top_value)


def setup_inputs(seed: int = 0) -> dict:
    arg_keys = jax.random.split(jax.random.key(seed), 5)
    return {
        "codes": draw_codes(jax.random.fold_in(arg_keys[4], 71), 0),
        "cand_hidden": draw_cand_hidden(jax.random.fold_in(arg_keys[4], 71), 0),
        "proj": draw_proj(jax.random.fold_in(arg_keys[4], 71), 0),
        "gold": set_ends(jax.random.randint(arg_keys[3], (CONTEXTS,), 0, B * N_LOOP), jax.random.fold_in(arg_keys[3], 1), 0, (B * N_LOOP) - 1).astype(jnp.int32),
    }


def regroup(array):
    shape = array.shape[1:]
    split = array.reshape((N_LOOP, N_DP, B) + shape)
    moved = jnp.swapaxes(split, 0, 1)
    return moved.reshape((N_DP, N_LOOP * B) + shape)


def ungroup(array):
    shape = array.shape[2:]
    split = array.reshape((N_DP, N_LOOP, B) + shape)
    moved = jnp.swapaxes(split, 0, 1)
    return moved.reshape((N_LOOP * N_DP * B,) + shape)


def reference(codes, cand_hidden, proj, gold):
    inv_scale = D ** -0.5

    def one_group(inputs):
        group_codes, group_hidden, group_gold = inputs
        count = group_hidden.shape[0]
        cand_embed = jnp.dot(group_hidden, proj, preferred_element_type=jnp.float32).astype(jnp.bfloat16)
        code_rows = group_codes.reshape(count * M, D)
        raw = lax.dot_general(cand_embed, code_rows, (((1,), (1,)), ((), ())), preferred_element_type=jnp.float32)
        logits = raw.reshape(count, count, M) * inv_scale
        top_logit = jnp.max(logits, axis=-1, keepdims=True)
        weights = jnp.exp(logits - top_logit)
        probs = weights / jnp.sum(weights, axis=-1, keepdims=True)
        scores = jnp.sum(probs * logits, axis=-1)
        top_score = jnp.max(scores, axis=0)
        log_total = top_score + jnp.log(jnp.sum(jnp.exp(scores - top_score[None, :]), axis=0))
        cand_ids = jnp.arange(count, dtype=jnp.int32)
        gold_hot = (cand_ids[:, None] == group_gold[None, :]).astype(jnp.float32)
        context_loss = log_total - jnp.sum(gold_hot * scores, axis=0)
        score_grad = jnp.exp(scores - log_total[None, :]) - gold_hot
        logit_grad = (score_grad[:, :, None] * probs * (1.0 + logits - scores[:, :, None]) * inv_scale).astype(jnp.bfloat16)
        logit_grad = logit_grad.reshape(count, count * M)
        code_grad = lax.dot_general(logit_grad, cand_embed, (((0,), (0,)), ((), ())), preferred_element_type=jnp.float32)
        embed_grad = jnp.dot(logit_grad, code_rows, preferred_element_type=jnp.float32).astype(jnp.bfloat16)
        proj_part = lax.dot_general(group_hidden, embed_grad, (((0,), (0,)), ((), ())), preferred_element_type=jnp.float32)
        return context_loss, code_grad.reshape(count, M, D), proj_part

    losses, code_grads, proj_parts = lax.map(one_group, (regroup(codes), regroup(cand_hidden), regroup(gold)))
    return ungroup(losses), ungroup(code_grads), jnp.sum(proj_parts, axis=0)
```

```python
import functools

import jax
import jax.numpy as jnp
from jax import lax
from jax.experimental import pallas as pl
from jax.experimental.pallas import tpu as pltpu
from jax.sharding import PartitionSpec as P

bf16, f32 = jnp.bfloat16, jnp.float32
NT = (((1,), (1,)), ((), ()))
NN = (((1,), (0,)), ((), ()))
TN = (((0,), (0,)), ((), ()))
MIB = 1024 * 1024

PLANE_GROUPS = [
    [(y * 4 + xl * 2 + c) * 16 + z * 2 + xh for y in range(4) for xl in range(2) for xh in range(2)]
    for z in range(8)
    for c in range(2)
]
Z_GROUPS = [[z * 2 + xh for z in range(8)] for xh in range(2)]


def dot(a, b, dims):
    return lax.dot_general(a, b, dims, preferred_element_type=f32)


def along_loop(value, to):
    return lax.ppermute(value, "loop", [(i, to(i)) for i in range(16)])


def other_core(value):
    return along_loop(value, lambda i: i ^ 1)


def other_x(value):
    return along_loop(value, lambda i: i ^ 2)


def from_y(value, by):
    return along_loop(value, lambda i: ((i // 4 - by) % 4) * 4 + i % 4)


def gather_chips(own):
    x_ = other_x(own)
    y1 = from_y(own, 1)
    y3 = from_y(own, -1)
    xy1 = other_x(y1)
    xy3 = from_y(x_, -1)
    y2 = from_y(y1, 1)
    xy2 = (other_x(y2[:32]), from_y(xy1[32:48], 1), from_y(xy3[48:], -1))
    return jnp.concatenate((own, y1, y2, y3, x_, xy1) + xy2 + (xy3,), axis=0)


def scores_kernel(codes_per, core_ref, c_ref, h0_ref, h1_ref, proj_ref, gold_ref,
                  loss_ref, lg_ref, e_ref, keep_ref, send_ref, raw, part, score, w):
    rows, width = c_ref.shape
    half = h0_ref.shape[0]
    cands = 2 * half
    inv_scale = width ** -0.5
    block = 256
    ctxs = block // codes_per
    lanes = 128
    for k in range(half // 256):
        s = slice(k * 256, (k + 1) * 256)
        e_ref[s, :] = dot(h0_ref[s, :], proj_ref[...], NN).astype(bf16)
    for k in range(half // 256):
        s = slice(k * 256, (k + 1) * 256)
        e_ref[half + k * 256 : half + (k + 1) * 256, :] = dot(h1_ref[s, :], proj_ref[...], NN).astype(bf16)
    for b in range(rows // block):
        s = slice(b * block, (b + 1) * block)
        cs = slice(b * ctxs, (b + 1) * ctxs)
        raw[b % 2] = dot(c_ref[s, :], e_ref[...], NT)
        for i in range(ctxs // 8):
            sub = slice(i * 8 * codes_per, (i + 1) * 8 * codes_per)
            at = slice(b * ctxs + i * 8, b * ctxs + i * 8 + 8)
            for q in range(cands // lanes):
                ls = slice(q * lanes, (q + 1) * lanes)
                logit = raw[b % 2, sub, ls].reshape(8, codes_per, lanes) * inv_scale
                weight = jnp.exp(logit - jnp.max(logit, axis=1, keepdims=True))
                prob = weight * (1.0 / jnp.sum(weight, axis=1, keepdims=True))
                mean = jnp.sum(prob * logit, axis=1, keepdims=True)
                slope = prob * (1.0 + logit - mean) * inv_scale
                part[b % 2, sub, ls] = slope.reshape(8 * codes_per, lanes)
                score[at, ls] = mean.reshape(8, lanes)
        mine = score[cs, :]
        top = jnp.max(mine, axis=1, keepdims=True)
        log_total = top + jnp.log(jnp.sum(jnp.exp(mine - top), axis=1, keepdims=True))
        hot = (lax.broadcasted_iota(jnp.int32, (ctxs, cands), 1) == gold_ref[cs, :]).astype(f32)
        loss_ref[cs, :] = log_total - jnp.sum(hot * mine, axis=1, keepdims=True)
        score_grad = jnp.exp(mine - log_total) - hot
        for q in range(cands // lanes):
            ls = slice(q * lanes, (q + 1) * lanes)
            grad = part[b % 2, :, ls].reshape(ctxs, codes_per, lanes) * score_grad[:, None, ls]
            lg_ref[s, ls] = grad.reshape(block, lanes).astype(bf16)
        w[s, :] = (dot(lg_ref[s, :half], h0_ref[...], NN) + dot(lg_ref[s, half:], h1_ref[...], NN)).astype(bf16)
    first_core = core_ref[0] == 0
    for k in range(width // 256):
        both = dot(w[:, k * 256 : (k + 1) * 256], c_ref[...], TN)
        for n in range(2):
            pair = []
            for c in range(2):
                piece = both[n * 128 + c * 64 : n * 128 + (c + 1) * 64].reshape(4, 16, width)
                low, high = piece[:, :8], piece[:, 8:]
                pair.append([
                    jnp.concatenate((low[:, :4], high[:, :4]), axis=1).reshape(32, width),
                    jnp.concatenate((low[:, 4:], high[:, 4:]), axis=1).reshape(32, width),
                ])
            for xh in range(2):
                to = (k * 2 + n) * 2 + xh
                keep_ref[to] = jnp.where(first_core, pair[0][xh], pair[1][xh])
                send_ref[to] = jnp.where(first_core, pair[1][xh], pair[0][xh]).astype(bf16)


def scores_call(core, code_rows, h0, h1, proj, gold, codes_per):
    rows, width = code_rows.shape
    ctxs = rows // codes_per
    cands = 2 * h0.shape[0]
    vmem = pl.BlockSpec(memory_space=pltpu.VMEM)
    shape = jax.ShapeDtypeStruct
    return pl.pallas_call(
        functools.partial(scores_kernel, codes_per),
        out_shape=(
            shape((ctxs, 1), f32),
            shape((rows, cands), bf16),
            shape((cands, width), bf16),
            shape((16, 32, width), f32),
            shape((16, 32, width), bf16),
        ),
        in_specs=[pl.BlockSpec(memory_space=pltpu.SMEM)] + [vmem] * 5,
        out_specs=(vmem,) * 5,
        scratch_shapes=[
            pltpu.VMEM((2, 256, cands), f32),
            pltpu.VMEM((2, 256, cands), f32),
            pltpu.VMEM((ctxs, cands), f32),
            pltpu.VMEM((rows, width), bf16),
        ],
        compiler_params=pltpu.CompilerParams(vmem_limit_bytes=16 * MIB),
        cost_estimate=pl.CostEstimate(flops=2 * 4 * 1024**3, bytes_accessed=10 * MIB, transcendentals=1024**2),
        name="scores_and_grads",
    )(core, code_rows, h0, h1, proj, gold)


def code_grad_kernel(lg_ref, e_ref, o_ref):
    o_ref[...] = dot(lg_ref[...], e_ref[...], NN)


def code_grad_call(lg, e):
    rows, width = lg.shape[0], e.shape[1]
    return pl.pallas_call(
        code_grad_kernel,
        grid=(rows // 256,),
        out_shape=jax.ShapeDtypeStruct((rows, width), f32),
        in_specs=[pl.BlockSpec((256, lg.shape[1]), lambda i: (i, 0)), pl.BlockSpec(e.shape, lambda i: (0, 0))],
        out_specs=pl.BlockSpec((256, width), lambda i: (i, 0)),
        compiler_params=pltpu.CompilerParams(vmem_limit_bytes=10 * MIB),
        cost_estimate=pl.CostEstimate(flops=2 * 1024**3, bytes_accessed=8 * MIB, transcendentals=0),
        name="code_grad",
    )(lg, e)


def local(codes, cand_hidden, proj, gold):
    ctxs, codes_per, width = codes.shape
    me = lax.axis_index("loop")
    y, x, core = me // 4, (me // 2) % 2, me % 2
    owner, place = gold // ctxs, gold % ctxs
    spot = ((owner % 2) ^ core) * 8 + (((owner // 2) % 2) ^ x) * 4 + (owner // 4 - y) % 4
    gold_at = (spot * ctxs + place)[:, None]
    h0 = gather_chips(cand_hidden)
    h1 = other_core(h0)
    loss, lg, e, keep, send = scores_call(
        core[None], codes.reshape(ctxs * codes_per, width), h0, h1, proj, gold_at, codes_per
    )
    got = other_core(send)
    code_grad = code_grad_call(lg, e)
    plane = lax.all_to_all(
        (keep + got.astype(f32)).astype(bf16), ("loop", "dp"), 0, 0, axis_index_groups=PLANE_GROUPS, tiled=True
    )
    plane, code_grad = lax.optimization_barrier((plane, code_grad))
    line = jnp.sum(plane.astype(f32), axis=0).astype(bf16).reshape(8, 4, width)
    last = lax.all_to_all(line, "dp", 0, 0, axis_index_groups=Z_GROUPS, tiled=True)
    proj_grad = jnp.sum(last.astype(f32), axis=0)
    return loss[:, 0], code_grad.reshape(ctxs, codes_per, width), proj_grad


def solution(mesh):
    return jax.shard_map(
        local,
        mesh=mesh,
        in_specs=(P(("loop", "dp"), None, None), P(("loop", "dp"), None), P(), P(("loop", "dp"))),
        out_specs=(P(("loop", "dp")), P(("loop", "dp"), None, None), P(("loop", "dp"), None)),
        check_vma=False,
    )
```

```python
import functools

import jax
import jax.numpy as jnp
from jax import lax
from jax.experimental import pallas as pl
from jax.experimental.pallas import tpu as pltpu
from jax.sharding import PartitionSpec as P

bf16, f32 = jnp.bfloat16, jnp.float32
NT = (((1,), (1,)), ((), ()))
NN = (((1,), (0,)), ((), ()))
TN = (((0,), (0,)), ((), ()))
MIB = 1024 * 1024

PLANE_GROUPS = [
    [(y * 4 + xl * 2 + c) * 16 + z * 2 + xh for y in range(4) for xl in range(2) for xh in range(2)]
    for z in range(8)
    for c in range(2)
]
Z_GROUPS = [[z * 2 + xh for z in range(8)] for xh in range(2)]


def dot(a, b, dims):
    return lax.dot_general(a, b, dims, preferred_element_type=f32)


def along_loop(value, to):
    return lax.ppermute(value, "loop", [(i, to(i)) for i in range(16)])


def other_core(value):
    return along_loop(value, lambda i: i ^ 1)


def other_x(value):
    return along_loop(value, lambda i: i ^ 2)


def other_y(value, by):
    return along_loop(value, lambda i: i ^ (4 * by))


def gather_chips(own):
    x_ = other_x(own)
    y1 = other_y(own, 1)
    y3 = other_y(own, 3)
    xy1 = other_x(y1)
    xy3 = other_y(x_, 3)
    y2 = other_y(y3, 1)
    xy2 = (other_x(y2[:32]), other_y(xy1[32:48], 3), other_y(xy3[48:], 1))
    return jnp.concatenate((own, y1, y2, y3, x_, xy1) + xy2 + (xy3,), axis=0)


def softmax_part(codes_per, c_ref, e_ref, slope_ref, mean_ref, raw):
    rows, width = c_ref.shape
    cands = e_ref.shape[0]
    inv_scale = width ** -0.5
    block, lanes = 256, 128
    ctxs = block // codes_per

    def logits(b):
        raw[b % 2] = dot(c_ref[b * block : (b + 1) * block], e_ref[...], NT)

    logits(0)
    for b in range(rows // block):
        if (b + 1) * block < rows:
            logits(b + 1)
        for i in range(ctxs // 8):
            sub = slice(i * 8 * codes_per, (i + 1) * 8 * codes_per)
            out = slice(b * block + sub.start, b * block + sub.stop)
            at = slice(b * ctxs + i * 8, b * ctxs + i * 8 + 8)
            for n in range(cands // lanes):
                ls = slice(n * lanes, (n + 1) * lanes)
                logit = raw[b % 2, sub, ls].reshape(8, codes_per, lanes) * inv_scale
                weight = jnp.exp(logit - jnp.max(logit, axis=1, keepdims=True))
                norm = 1.0 / jnp.sum(weight, axis=1, keepdims=True)
                mean = jnp.sum(weight * logit, axis=1, keepdims=True) * norm
                slope = weight * (1.0 + (logit - mean)) * (norm * inv_scale)
                slope_ref[out, ls] = slope.reshape(8 * codes_per, lanes)
                mean_ref[at, ls] = mean.reshape(8, lanes)


def part_kernel(codes_per, c_ref, proj_ref, *refs):
    h_refs, (h_ref, e_ref, slope_ref, mean_ref, raw) = refs[:-5], refs[-5:]
    start = 0
    for ref in h_refs:
        stop = start + ref.shape[0]
        h_ref[start:stop] = ref[...]
        start = stop
    for at in range(0, h_ref.shape[0], 256):
        e_ref[at : at + 256] = dot(h_ref[at : at + 256], proj_ref[...], NN).astype(bf16)
    softmax_part(codes_per, c_ref, e_ref, slope_ref, mean_ref, raw)


def part_call(code_rows, proj, pieces, codes_per, name):
    rows, width = code_rows.shape
    cands = sum(p.shape[0] for p in pieces)
    vmem = pl.BlockSpec(memory_space=pltpu.VMEM)
    shape = jax.ShapeDtypeStruct
    return pl.pallas_call(
        functools.partial(part_kernel, codes_per),
        out_shape=(
            shape((cands, width), bf16),
            shape((cands, width), bf16),
            shape((rows, cands), f32),
            shape((rows // codes_per, cands), f32),
        ),
        in_specs=[vmem] * (2 + len(pieces)),
        out_specs=(vmem,) * 4,
        scratch_shapes=[pltpu.VMEM((2, 256, cands), f32)],
        compiler_params=pltpu.CompilerParams(vmem_limit_bytes=8 * MIB),
        cost_estimate=pl.CostEstimate(flops=cands * 4 * 1024**2, bytes_accessed=6 * MIB, transcendentals=0),
        name=name,
    )(code_rows, proj, *pieces)


def scores_kernel(codes_per, core_ref, c_ref, *refs):
    gold_ref, loss_ref, lg_ref, keep_ref, send_ref, h, score, w = refs[-8:]
    parts = [refs[i : i + 3] for i in range(0, len(refs) - 8, 3)]
    rows, width = c_ref.shape
    block, lanes, cands = 256, 128, h.shape[0]
    blocks, ctxs = rows // block, block // codes_per
    slopes, start = [], 0
    for h_part, slope_part, mean_part in parts:
        stop = start + h_part.shape[0]
        h[start:stop] = h_part[...]
        score[:, start:stop] = mean_part[...]
        slopes += [(slope_part, at) for at in range(0, stop - start, lanes)]
        start = stop

    def loss_and_grads(b):
        cs = slice(b * ctxs, (b + 1) * ctxs)
        s = slice(b * block, (b + 1) * block)
        mine = score[cs, :]
        top = jnp.max(mine, axis=1, keepdims=True)
        log_total = top + jnp.log(jnp.sum(jnp.exp(mine - top), axis=1, keepdims=True))
        hot = (lax.broadcasted_iota(jnp.int32, (ctxs, cands), 1) == gold_ref[cs, :]).astype(f32)
        loss_ref[cs, :] = log_total - jnp.sum(hot * mine, axis=1, keepdims=True)
        score_grad = jnp.exp(mine - log_total) - hot
        for n in range(cands // lanes):
            slope_ref, at = slopes[n]
            slope = slope_ref[s, at : at + lanes].reshape(ctxs, codes_per, lanes)
            grad = slope * score_grad[:, None, n * lanes : (n + 1) * lanes]
            lg_ref[s, n * lanes : (n + 1) * lanes] = grad.reshape(block, lanes).astype(bf16)

    def weigh(b):
        s = slice(b * block, (b + 1) * block)
        w[s, :] = dot(lg_ref[s, :], h[...], NN).astype(bf16)

    loss_and_grads(0)
    for b in range(blocks):
        if b + 1 < blocks:
            loss_and_grads(b + 1)
        weigh(b)
    first_core = core_ref[0] == 0
    half = width // 2
    for k in range(width // 256):
        both = dot(w[:, k * 256 : (k + 1) * 256], c_ref[...], TN)
        for n in range(2):
            pair = []
            for c in range(2):
                piece = both[n * 128 + c * 64 : n * 128 + (c + 1) * 64].reshape(8, 8, width)
                left, right = piece[:, :, :half], piece[:, :, half:]
                pair.append([
                    jnp.concatenate((left[:, :4], right[:, :4]), axis=1).reshape(64, half),
                    jnp.concatenate((left[:, 4:], right[:, 4:]), axis=1).reshape(64, half),
                ])
            for xh in range(2):
                to = (k * 2 + n) * 2 + xh
                keep_ref[to] = jnp.where(first_core, pair[0][xh], pair[1][xh])
                send_ref[to] = jnp.where(first_core, pair[1][xh], pair[0][xh]).astype(bf16)


def scores_call(core, code_rows, parts, gold, codes_per):
    rows, width = code_rows.shape
    ctxs = rows // codes_per
    cands = sum(p[0].shape[0] for p in parts)
    vmem = pl.BlockSpec(memory_space=pltpu.VMEM)
    shape = jax.ShapeDtypeStruct
    return pl.pallas_call(
        functools.partial(scores_kernel, codes_per),
        out_shape=(
            shape((ctxs, 1), f32),
            shape((rows, cands), bf16),
            shape((16, 64, width // 2), f32),
            shape((16, 64, width // 2), bf16),
        ),
        in_specs=[pl.BlockSpec(memory_space=pltpu.SMEM)] + [vmem] * (2 + 3 * len(parts)),
        out_specs=(vmem,) * 4,
        scratch_shapes=[
            pltpu.VMEM((cands, width), bf16),
            pltpu.VMEM((ctxs, cands), f32),
            pltpu.VMEM((rows, width), bf16),
        ],
        compiler_params=pltpu.CompilerParams(vmem_limit_bytes=14 * MIB),
        cost_estimate=pl.CostEstimate(flops=2 * 2 * 1024**3, bytes_accessed=10 * MIB, transcendentals=1024),
        name="loss_and_grads",
    )(core, code_rows, *(x for p in parts for x in (p[0], p[2], p[3])), gold)


def code_grad_kernel(lg_ref, *refs):
    e_refs, o_ref = refs[:-1], refs[-1]
    total, start = 0.0, 0
    for ref in e_refs:
        stop = start + ref.shape[0]
        total = total + dot(lg_ref[:, start:stop], ref[...], NN)
        start = stop
    o_ref[...] = total


def code_grad_call(lg, es):
    rows, width = lg.shape[0], es[0].shape[1]
    return pl.pallas_call(
        code_grad_kernel,
        grid=(rows // 256,),
        out_shape=jax.ShapeDtypeStruct((rows, width), f32),
        in_specs=[pl.BlockSpec((256, lg.shape[1]), lambda i: (i, 0))]
        + [pl.BlockSpec(e.shape, lambda i: (0, 0)) for e in es],
        out_specs=pl.BlockSpec((256, width), lambda i: (i, 0)),
        compiler_params=pltpu.CompilerParams(vmem_limit_bytes=10 * MIB),
        cost_estimate=pl.CostEstimate(flops=2 * 1024**3, bytes_accessed=8 * MIB, transcendentals=0),
        name="code_grad",
    )(lg, *es)


def local(codes, cand_hidden, proj, gold):
    ctxs, codes_per, width = codes.shape
    me = lax.axis_index("loop")
    y, x, core = me // 4, (me // 2) % 2, me % 2
    owner, place = gold // ctxs, gold % ctxs
    spot = ((owner % 2) ^ core) * 8 + (((owner // 2) % 2) ^ x) * 4 + ((owner // 4) ^ y)
    gold_at = (spot * ctxs + place)[:, None]
    code_rows = codes.reshape(ctxs * codes_per, width)
    h0 = gather_chips(cand_hidden)
    h1 = other_core(h0)
    parts = [
        part_call(code_rows, proj, (h,), codes_per, name) for h, name in ((h0, "part_near"), (h1, "part_far"))
    ]
    loss, lg, keep, send = scores_call(core[None], code_rows, parts, gold_at, codes_per)
    got = other_core(send)
    code_grad = code_grad_call(lg, [p[1] for p in parts])
    plane = lax.all_to_all((keep + got.astype(f32)).astype(bf16), ("loop", "dp"), 0, 0, axis_index_groups=PLANE_GROUPS, tiled=True)
    plane, code_grad = lax.optimization_barrier((plane, code_grad))
    line = jnp.sum(plane.astype(f32), axis=0).astype(bf16).reshape(8, 8, width // 2)
    last = lax.all_to_all(line, "dp", 0, 0, axis_index_groups=Z_GROUPS, tiled=True)
    proj_rows = jnp.sum(last.astype(f32), axis=0)
    proj_grad = jnp.concatenate((proj_rows[:4], proj_rows[4:]), axis=1)
    return loss[:, 0], code_grad.reshape(ctxs, codes_per, width), proj_grad


def solution(mesh):
    return jax.shard_map(
        local,
        mesh=mesh,
        in_specs=(P(("loop", "dp"), None, None), P(("loop", "dp"), None), P(), P(("loop", "dp"))),
        out_specs=(P(("loop", "dp")), P(("loop", "dp"), None, None), P(("loop", "dp"), None)),
        check_vma=False,
    )
```

```python
import functools

import jax
import jax.numpy as jnp
from jax import lax
from jax.experimental import pallas as pl
from jax.experimental.pallas import tpu as pltpu
from jax.sharding import PartitionSpec as P

bf16, f32 = jnp.bfloat16, jnp.float32
NT = (((1,), (1,)), ((), ()))
NN = (((1,), (0,)), ((), ()))
TN = (((0,), (0,)), ((), ()))
MIB = 1024 * 1024

PLANE_GROUPS = [
    [(y * 4 + xl * 2 + c) * 16 + z * 2 + xh for y in range(4) for xl in range(2) for xh in range(2)]
    for z in range(8)
    for c in range(2)
]
Z_GROUPS = [[z * 2 + xh for z in range(8)] for xh in range(2)]


def dot(a, b, dims):
    return lax.dot_general(a, b, dims, preferred_element_type=f32)


def along_loop(value, to):
    return lax.ppermute(value, "loop", [(i, to(i)) for i in range(16)])


def other_core(value):
    return along_loop(value, lambda i: i ^ 1)


def other_x(value):
    return along_loop(value, lambda i: i ^ 2)


def other_y(value, by):
    return along_loop(value, lambda i: i ^ (4 * by))


def gather_chips(own):
    x_ = other_x(own)
    y1 = other_y(own, 1)
    y3 = other_y(own, 3)
    xy1 = other_x(y1)
    xy3 = other_y(x_, 3)
    y2 = other_y(y3, 1)
    return jnp.concatenate((own, y1, y2, y3, x_, xy1, other_x(y2), xy3), axis=0)


def combine_kernel(keep_ref, got_ref, o_any, total, sems):
    copies = []
    for q in range(4):
        part = slice(q * 4, (q + 1) * 4)
        total[part] = (keep_ref[part] + got_ref[part].astype(f32)).astype(bf16)
        copies.append(pltpu.make_async_copy(total.at[part], o_any.at[part], sems.at[q]))
        copies[-1].start()
    for copy in copies:
        copy.wait()


def combine_call(keep, got):
    vmem = pl.BlockSpec(memory_space=pltpu.VMEM)
    return pl.pallas_call(
        combine_kernel,
        out_shape=jax.ShapeDtypeStruct(got.shape, bf16),
        in_specs=[vmem, vmem],
        out_specs=pl.BlockSpec(memory_space=pltpu.HBM),
        scratch_shapes=[pltpu.VMEM(got.shape, bf16), pltpu.SemaphoreType.DMA((4,))],
        compiler_params=pltpu.CompilerParams(vmem_limit_bytes=8 * MIB),
        name="combine",
    )(keep, got)


def softmax_part(codes_per, c_ref, e_ref, slope_ref, mean_ref, raw):
    rows, width = c_ref.shape
    cands = e_ref.shape[0]
    inv_scale = width ** -0.5
    block, lanes = 256, 128
    ctxs = block // codes_per

    def logits(b):
        raw[b % 2] = dot(c_ref[b * block : (b + 1) * block], e_ref[...], NT)

    logits(0)
    for b in range(rows // block):
        if (b + 1) * block < rows:
            logits(b + 1)
        for i in range(ctxs // 8):
            sub = slice(i * 8 * codes_per, (i + 1) * 8 * codes_per)
            out = slice(b * block + sub.start, b * block + sub.stop)
            at = slice(b * ctxs + i * 8, b * ctxs + i * 8 + 8)
            for n in range(cands // lanes):
                ls = slice(n * lanes, (n + 1) * lanes)
                logit = raw[b % 2, sub, ls].reshape(8, codes_per, lanes) * inv_scale
                weight = jnp.exp(logit - jnp.max(logit, axis=1, keepdims=True))
                norm = 1.0 / jnp.sum(weight, axis=1, keepdims=True)
                mean = jnp.sum(weight * logit, axis=1, keepdims=True) * norm
                slope = weight * (1.0 + (logit - mean)) * (norm * inv_scale)
                slope_ref[out, ls] = slope.reshape(8 * codes_per, lanes)
                mean_ref[at, ls] = mean.reshape(8, lanes)


def part_kernel(codes_per, c_ref, proj_ref, *refs):
    h_refs, (h_ref, slope_ref, mean_ref, e_ref, raw) = refs[:-5], refs[-5:]
    start = 0
    for ref in h_refs:
        stop = start + ref.shape[0]
        h_ref[start:stop] = ref[...]
        start = stop
    for at in range(0, h_ref.shape[0], 256):
        e_ref[at : at + 256] = dot(h_ref[at : at + 256], proj_ref[...], NN).astype(bf16)
    softmax_part(codes_per, c_ref, e_ref, slope_ref, mean_ref, raw)


def part_call(code_rows, proj, pieces, codes_per, name):
    rows, width = code_rows.shape
    cands = sum(p.shape[0] for p in pieces)
    vmem = pl.BlockSpec(memory_space=pltpu.VMEM)
    shape = jax.ShapeDtypeStruct
    return pl.pallas_call(
        functools.partial(part_kernel, codes_per),
        out_shape=(
            shape((cands, width), bf16),
            shape((rows, cands), f32),
            shape((rows // codes_per, cands), f32),
        ),
        in_specs=[vmem] * (2 + len(pieces)),
        out_specs=(vmem,) * 3,
        scratch_shapes=[pltpu.VMEM((cands, width), bf16), pltpu.VMEM((2, 256, cands), f32)],
        compiler_params=pltpu.CompilerParams(vmem_limit_bytes=8 * MIB),
        cost_estimate=pl.CostEstimate(flops=cands * 4 * 1024**2, bytes_accessed=6 * MIB, transcendentals=0),
        name=name,
    )(code_rows, proj, *pieces)


def scores_kernel(codes_per, core_ref, c_ref, *refs):
    gold_ref, loss_ref, w, keep_ref, send_ref, h, score, lg_ref = refs[-8:]
    parts = [refs[i : i + 3] for i in range(0, len(refs) - 8, 3)]
    rows, width = c_ref.shape
    block, lanes, cands = 256, 128, h.shape[0]
    blocks, ctxs = rows // block, block // codes_per
    slopes, start = [], 0
    for h_part, slope_part, mean_part in parts:
        stop = start + h_part.shape[0]
        h[start:stop] = h_part[...]
        score[:, start:stop] = mean_part[...]
        slopes += [(slope_part, at) for at in range(0, stop - start, lanes)]
        start = stop

    def loss_and_grads(b):
        cs = slice(b * ctxs, (b + 1) * ctxs)
        s = slice(b * block, (b + 1) * block)
        mine = score[cs, :]
        top = jnp.max(mine, axis=1, keepdims=True)
        log_total = top + jnp.log(jnp.sum(jnp.exp(mine - top), axis=1, keepdims=True))
        hot = (lax.broadcasted_iota(jnp.int32, (ctxs, cands), 1) == gold_ref[cs, :]).astype(f32)
        loss_ref[cs, :] = log_total - jnp.sum(hot * mine, axis=1, keepdims=True)
        score_grad = jnp.exp(mine - log_total) - hot
        for n in range(cands // lanes):
            slope_ref, at = slopes[n]
            slope = slope_ref[s, at : at + lanes].reshape(ctxs, codes_per, lanes)
            grad = slope * score_grad[:, None, n * lanes : (n + 1) * lanes]
            lg_ref[s, n * lanes : (n + 1) * lanes] = grad.reshape(block, lanes).astype(bf16)

    def weigh(b):
        s = slice(b * block, (b + 1) * block)
        w[s, :] = dot(lg_ref[s, :], h[...], NN).astype(bf16)

    loss_and_grads(0)
    for b in range(blocks):
        if b + 1 < blocks:
            loss_and_grads(b + 1)
        weigh(b)
    first_core = core_ref[0] == 0
    half = width // 2
    for k in range(width // 256):
        both = dot(w[:, k * 256 : (k + 1) * 256], c_ref[...], TN)
        for n in range(2):
            pair = []
            for c in range(2):
                piece = both[n * 128 + c * 64 : n * 128 + (c + 1) * 64].reshape(8, 8, width)
                left, right = piece[:, :, :half], piece[:, :, half:]
                pair.append([
                    jnp.concatenate((left[:, :4], right[:, :4]), axis=1).reshape(64, half),
                    jnp.concatenate((left[:, 4:], right[:, 4:]), axis=1).reshape(64, half),
                ])
            for xh in range(2):
                to = (k * 2 + n) * 2 + xh
                keep_ref[to] = jnp.where(first_core, pair[0][xh], pair[1][xh])
                send_ref[to] = jnp.where(first_core, pair[1][xh], pair[0][xh]).astype(bf16)


def scores_call(core, code_rows, parts, gold, codes_per):
    rows, width = code_rows.shape
    ctxs = rows // codes_per
    cands = sum(p[0].shape[0] for p in parts)
    vmem = pl.BlockSpec(memory_space=pltpu.VMEM)
    shape = jax.ShapeDtypeStruct
    return pl.pallas_call(
        functools.partial(scores_kernel, codes_per),
        out_shape=(
            shape((ctxs, 1), f32),
            shape((rows, width), bf16),
            shape((16, 64, width // 2), f32),
            shape((16, 64, width // 2), bf16),
        ),
        in_specs=[pl.BlockSpec(memory_space=pltpu.SMEM)] + [vmem] * (2 + 3 * len(parts)),
        out_specs=(vmem,) * 4,
        scratch_shapes=[
            pltpu.VMEM((cands, width), bf16),
            pltpu.VMEM((ctxs, cands), f32),
            pltpu.VMEM((rows, cands), bf16),
        ],
        compiler_params=pltpu.CompilerParams(vmem_limit_bytes=8 * MIB),
        cost_estimate=pl.CostEstimate(flops=2 * 2 * 1024**3, bytes_accessed=10 * MIB, transcendentals=1024),
        name="loss_and_grads",
    )(core, code_rows, *(x for p in parts for x in p), gold)


def code_grad_kernel(w_ref, proj_ref, o_ref):
    o_ref[...] = dot(w_ref[...], proj_ref[...], NN)


def code_grad_call(w, proj):
    rows, width = w.shape[0], proj.shape[1]
    return pl.pallas_call(
        code_grad_kernel,
        grid=(rows // 256,),
        out_shape=jax.ShapeDtypeStruct((rows, width), f32),
        in_specs=[pl.BlockSpec((256, w.shape[1]), lambda i: (i, 0)), pl.BlockSpec(proj.shape, lambda i: (0, 0))],
        out_specs=pl.BlockSpec((256, width), lambda i: (i, 0)),
        compiler_params=pltpu.CompilerParams(vmem_limit_bytes=10 * MIB),
        cost_estimate=pl.CostEstimate(flops=2 * 1024**3, bytes_accessed=8 * MIB, transcendentals=0),
        name="code_grad",
    )(w, proj)


def local(codes, cand_hidden, proj, gold):
    ctxs, codes_per, width = codes.shape
    me = lax.axis_index("loop")
    y, x, core = me // 4, (me // 2) % 2, me % 2
    owner, place = gold // ctxs, gold % ctxs
    spot = ((owner % 2) ^ core) * 8 + (((owner // 2) % 2) ^ x) * 4 + ((owner // 4) ^ y)
    gold_at = (spot * ctxs + place)[:, None]
    code_rows = codes.reshape(ctxs * codes_per, width)
    h0 = gather_chips(cand_hidden)
    h1 = other_core(h0)
    parts = [
        part_call(code_rows, proj, (h,), codes_per, name) for h, name in ((h0, "part_near"), (h1, "part_far"))
    ]
    loss, weighed, keep, send = scores_call(core[None], code_rows, parts, gold_at, codes_per)
    got = other_core(send)
    code_grad = code_grad_call(weighed, proj)
    plane = lax.all_to_all(combine_call(keep, got), ("loop", "dp"), 0, 0, axis_index_groups=PLANE_GROUPS, tiled=True)
    plane, code_grad = lax.optimization_barrier((plane, code_grad))
    line = jnp.sum(plane.astype(f32), axis=0).astype(bf16).reshape(8, 8, width // 2)
    last = lax.all_to_all(line, "dp", 0, 0, axis_index_groups=Z_GROUPS, tiled=True)
    proj_rows = jnp.sum(last.astype(f32), axis=0)
    proj_grad = jnp.concatenate((proj_rows[:4], proj_rows[4:]), axis=1)
    return loss[:, 0], code_grad.reshape(ctxs, codes_per, width), proj_grad


def solution(mesh):
    return jax.shard_map(
        local,
        mesh=mesh,
        in_specs=(P(("loop", "dp"), None, None), P(("loop", "dp"), None), P(), P(("loop", "dp"))),
        out_specs=(P(("loop", "dp")), P(("loop", "dp"), None, None), P(("loop", "dp"), None)),
        check_vma=False,
    )
```

```python
import functools

import jax
import jax.numpy as jnp
from jax import lax
from jax.experimental import pallas as pl
from jax.experimental.pallas import tpu as pltpu
from jax.sharding import PartitionSpec as P

bf16, f32 = jnp.bfloat16, jnp.float32
NT = (((1,), (1,)), ((), ()))
NN = (((1,), (0,)), ((), ()))
TN = (((0,), (0,)), ((), ()))
MIB = 1024 * 1024

PLANE_GROUPS = [
    [(y * 4 + xl * 2 + c) * 16 + z * 2 + xh for y in range(4) for xl in range(2) for xh in range(2)]
    for z in range(8)
    for c in range(2)
]
Z_GROUPS = [[z * 2 + xh for z in range(8)] for xh in range(2)]


def dot(a, b, dims):
    return lax.dot_general(a, b, dims, preferred_element_type=f32)


def along_loop(value, to):
    return lax.ppermute(value, "loop", [(i, to(i)) for i in range(16)])


def other_core(value):
    return along_loop(value, lambda i: i ^ 1)


def other_x(value):
    return along_loop(value, lambda i: i ^ 2)


def other_y(value, by):
    return along_loop(value, lambda i: i ^ (4 * by))


def gather_chips(own):
    x_ = other_x(own)
    y1 = other_y(own, 1)
    y3 = other_y(own, 3)
    xy1 = other_x(y1)
    xy3 = other_y(x_, 3)
    y2 = other_y(y3, 1)
    return jnp.concatenate((own, y1, y2, y3, x_, xy1, other_x(y2), xy3), axis=0)


def combine_kernel(keep_ref, got_ref, o_any, total, sems):
    copies = []
    for q in range(4):
        part = slice(q * 4, (q + 1) * 4)
        total[part] = (keep_ref[part] + got_ref[part].astype(f32)).astype(bf16)
        copies.append(pltpu.make_async_copy(total.at[part], o_any.at[part], sems.at[q]))
        copies[-1].start()
    for copy in copies:
        copy.wait()


def combine_call(keep, got):
    vmem = pl.BlockSpec(memory_space=pltpu.VMEM)
    return pl.pallas_call(
        combine_kernel,
        out_shape=jax.ShapeDtypeStruct(got.shape, bf16),
        in_specs=[vmem, vmem],
        out_specs=pl.BlockSpec(memory_space=pltpu.HBM),
        scratch_shapes=[pltpu.VMEM(got.shape, bf16), pltpu.SemaphoreType.DMA((4,))],
        compiler_params=pltpu.CompilerParams(vmem_limit_bytes=8 * MIB),
        name="combine",
    )(keep, got)


def softmax_part(codes_per, c_ref, e_ref, slope_ref, mean_ref, raw):
    rows, width = c_ref.shape
    cands = e_ref.shape[0]
    inv_scale = width ** -0.5
    block, lanes = 256, 128
    ctxs = block // codes_per

    def logits(b):
        raw[b % 2] = dot(c_ref[b * block : (b + 1) * block], e_ref[...], NT)

    logits(0)
    for b in range(rows // block):
        if (b + 1) * block < rows:
            logits(b + 1)
        for i in range(ctxs // 8):
            sub = slice(i * 8 * codes_per, (i + 1) * 8 * codes_per)
            out = slice(b * block + sub.start, b * block + sub.stop)
            at = slice(b * ctxs + i * 8, b * ctxs + i * 8 + 8)
            for n in range(cands // lanes):
                ls = slice(n * lanes, (n + 1) * lanes)
                logit = raw[b % 2, sub, ls].reshape(8, codes_per, lanes) * inv_scale
                weight = jnp.exp(logit - jnp.max(logit, axis=1, keepdims=True))
                norm = 1.0 / jnp.sum(weight, axis=1, keepdims=True)
                mean = jnp.sum(weight * logit, axis=1, keepdims=True) * norm
                slope = weight * (1.0 + (logit - mean)) * (norm * inv_scale)
                slope_ref[out, ls] = slope.reshape(8 * codes_per, lanes)
                mean_ref[at, ls] = mean.reshape(8, lanes)


def part_kernel(codes_per, c_ref, proj_ref, *refs):
    h_refs, (h_ref, slope_ref, mean_ref, e_ref, raw) = refs[:-5], refs[-5:]
    start = 0
    for ref in h_refs:
        stop = start + ref.shape[0]
        h_ref[start:stop] = ref[...]
        start = stop
    for at in range(0, h_ref.shape[0], 256):
        e_ref[at : at + 256] = dot(h_ref[at : at + 256], proj_ref[...], NN).astype(bf16)
    softmax_part(codes_per, c_ref, e_ref, slope_ref, mean_ref, raw)


def part_call(code_rows, proj, pieces, codes_per, name):
    rows, width = code_rows.shape
    cands = sum(p.shape[0] for p in pieces)
    vmem = pl.BlockSpec(memory_space=pltpu.VMEM)
    shape = jax.ShapeDtypeStruct
    return pl.pallas_call(
        functools.partial(part_kernel, codes_per),
        out_shape=(
            shape((cands, width), bf16),
            shape((rows, cands), f32),
            shape((rows // codes_per, cands), f32),
        ),
        in_specs=[vmem] * (2 + len(pieces)),
        out_specs=(vmem,) * 3,
        scratch_shapes=[pltpu.VMEM((cands, width), bf16), pltpu.VMEM((2, 256, cands), f32)],
        compiler_params=pltpu.CompilerParams(vmem_limit_bytes=8 * MIB),
        cost_estimate=pl.CostEstimate(flops=cands * 4 * 1024**2, bytes_accessed=6 * MIB, transcendentals=0),
        name=name,
    )(code_rows, proj, *pieces)


def scores_kernel(codes_per, rows, *refs):
    gold_ref, loss_ref, w, h, score, lg_ref = refs[-6:]
    parts = [refs[i : i + 3] for i in range(0, len(refs) - 6, 3)]
    block, lanes, cands = 256, 128, h.shape[0]
    blocks, ctxs = rows // block, block // codes_per
    slopes, start = [], 0
    for h_part, slope_part, mean_part in parts:
        stop = start + h_part.shape[0]
        h[start:stop] = h_part[...]
        score[:, start:stop] = mean_part[...]
        slopes += [(slope_part, at) for at in range(0, stop - start, lanes)]
        start = stop

    def loss_and_grads(b):
        cs = slice(b * ctxs, (b + 1) * ctxs)
        s = slice(b * block, (b + 1) * block)
        mine = score[cs, :]
        top = jnp.max(mine, axis=1, keepdims=True)
        log_total = top + jnp.log(jnp.sum(jnp.exp(mine - top), axis=1, keepdims=True))
        hot = (lax.broadcasted_iota(jnp.int32, (ctxs, cands), 1) == gold_ref[cs, :]).astype(f32)
        loss_ref[cs, :] = log_total - jnp.sum(hot * mine, axis=1, keepdims=True)
        score_grad = jnp.exp(mine - log_total) - hot
        for n in range(cands // lanes):
            slope_ref, at = slopes[n]
            slope = slope_ref[s, at : at + lanes].reshape(ctxs, codes_per, lanes)
            grad = slope * score_grad[:, None, n * lanes : (n + 1) * lanes]
            lg_ref[s, n * lanes : (n + 1) * lanes] = grad.reshape(block, lanes).astype(bf16)

    def weigh(b):
        s = slice(b * block, (b + 1) * block)
        w[s, :] = dot(lg_ref[s, :], h[...], NN).astype(bf16)

    loss_and_grads(0)
    for b in range(blocks):
        if b + 1 < blocks:
            loss_and_grads(b + 1)
        weigh(b)


def outer_kernel(core_ref, c_ref, w, keep_ref, send_ref):
    width = c_ref.shape[1]
    first_core = core_ref[0] == 0
    half = width // 2
    for k in range(width // 256):
        both = dot(w[:, k * 256 : (k + 1) * 256], c_ref[...], TN)
        for n in range(2):
            pair = []
            for c in range(2):
                piece = both[n * 128 + c * 64 : n * 128 + (c + 1) * 64].reshape(8, 8, width)
                left, right = piece[:, :, :half], piece[:, :, half:]
                pair.append([
                    jnp.concatenate((left[:, :4], right[:, :4]), axis=1).reshape(64, half),
                    jnp.concatenate((left[:, 4:], right[:, 4:]), axis=1).reshape(64, half),
                ])
            for xh in range(2):
                to = (k * 2 + n) * 2 + xh
                keep_ref[to] = jnp.where(first_core, pair[0][xh], pair[1][xh])
                send_ref[to] = jnp.where(first_core, pair[1][xh], pair[0][xh]).astype(bf16)


def scores_call(rows, parts, gold, codes_per):
    ctxs = rows // codes_per
    cands, width = sum(p[0].shape[0] for p in parts), parts[0][0].shape[1]
    vmem = pl.BlockSpec(memory_space=pltpu.VMEM)
    shape = jax.ShapeDtypeStruct
    return pl.pallas_call(
        functools.partial(scores_kernel, codes_per, rows),
        out_shape=(shape((ctxs, 1), f32), shape((rows, width), bf16)),
        in_specs=[vmem] * (1 + 3 * len(parts)),
        out_specs=(vmem,) * 2,
        scratch_shapes=[
            pltpu.VMEM((cands, width), bf16),
            pltpu.VMEM((ctxs, cands), f32),
            pltpu.VMEM((rows, cands), bf16),
        ],
        compiler_params=pltpu.CompilerParams(vmem_limit_bytes=8 * MIB),
        cost_estimate=pl.CostEstimate(flops=2 * 1024**3, bytes_accessed=8 * MIB, transcendentals=1024),
        name="loss_and_weigh",
    )(*(x for p in parts for x in p), gold)


def outer_call(core, code_rows, weighed):
    width = code_rows.shape[1]
    vmem = pl.BlockSpec(memory_space=pltpu.VMEM)
    shape = jax.ShapeDtypeStruct
    return pl.pallas_call(
        outer_kernel,
        out_shape=(shape((16, 64, width // 2), f32), shape((16, 64, width // 2), bf16)),
        in_specs=[pl.BlockSpec(memory_space=pltpu.SMEM), vmem, vmem],
        out_specs=(vmem,) * 2,
        compiler_params=pltpu.CompilerParams(vmem_limit_bytes=8 * MIB),
        cost_estimate=pl.CostEstimate(flops=2 * 1024**3, bytes_accessed=8 * MIB, transcendentals=0),
        name="outer",
    )(core, code_rows, weighed)


def code_grad_kernel(w_ref, proj_ref, o_ref):
    o_ref[...] = dot(w_ref[...], proj_ref[...], NN)


def code_grad_call(w, proj):
    rows, width = w.shape[0], proj.shape[1]
    return pl.pallas_call(
        code_grad_kernel,
        grid=(rows // 256,),
        out_shape=jax.ShapeDtypeStruct((rows, width), f32),
        in_specs=[pl.BlockSpec((256, w.shape[1]), lambda i: (i, 0)), pl.BlockSpec(proj.shape, lambda i: (0, 0))],
        out_specs=pl.BlockSpec((256, width), lambda i: (i, 0)),
        compiler_params=pltpu.CompilerParams(vmem_limit_bytes=10 * MIB),
        cost_estimate=pl.CostEstimate(flops=2 * 1024**3, bytes_accessed=8 * MIB, transcendentals=0),
        name="code_grad",
    )(w, proj)


def local(codes, cand_hidden, proj, gold):
    ctxs, codes_per, width = codes.shape
    me = lax.axis_index("loop")
    y, x, core = me // 4, (me // 2) % 2, me % 2
    owner, place = gold // ctxs, gold % ctxs
    spot = ((owner % 2) ^ core) * 8 + (((owner // 2) % 2) ^ x) * 4 + ((owner // 4) ^ y)
    gold_at = (spot * ctxs + place)[:, None]
    code_rows = codes.reshape(ctxs * codes_per, width)
    h0 = gather_chips(cand_hidden)
    h1 = other_core(h0)
    parts = [
        part_call(code_rows, proj, (h,), codes_per, name) for h, name in ((h0, "part_near"), (h1, "part_far"))
    ]
    loss, weighed = scores_call(ctxs * codes_per, parts, gold_at, codes_per)
    keep, send = outer_call(core[None], code_rows, weighed)
    got = other_core(send)
    code_grad = code_grad_call(weighed, proj)
    plane = lax.all_to_all(combine_call(keep, got), ("loop", "dp"), 0, 0, axis_index_groups=PLANE_GROUPS, tiled=True)
    plane, code_grad = lax.optimization_barrier((plane, code_grad))
    line = jnp.sum(plane.astype(f32), axis=0).astype(bf16).reshape(8, 8, width // 2)
    last = lax.all_to_all(line, "dp", 0, 0, axis_index_groups=Z_GROUPS, tiled=True)
    proj_rows = jnp.sum(last.astype(f32), axis=0)
    proj_grad = jnp.concatenate((proj_rows[:4], proj_rows[4:]), axis=1)
    return loss[:, 0], code_grad.reshape(ctxs, codes_per, width), proj_grad


def solution(mesh):
    return jax.shard_map(
        local,
        mesh=mesh,
        in_specs=(P(("loop", "dp"), None, None), P(("loop", "dp"), None), P(), P(("loop", "dp"))),
        out_specs=(P(("loop", "dp")), P(("loop", "dp"), None, None), P(("loop", "dp"), None)),
        check_vma=False,
    )
```
